256 devices in a mesh: row: 8 (over z), col: 32 (over x, y, core).
Axes of the slice: x: 4, y: 4, z: 8, core: 2. Of those that a mesh axis runs over, the one named last changes fastest.
Arguments:
- activations: bfloat16 [2, 512, 24, 24, 512], P(None, ('row', 'col')), may hold values from -6 to 6
- out_grads: bfloat16 [2, 512, 24, 24, 256], P(None, ('row', 'col')), may hold values from -6 to 6
- errors: bfloat16 [2, 1179648, 256], P(None, ('row', 'col')), may hold values from -10 to 10
- q_start: float32 [2, 256, 8], replicated, may hold values from -6 to 6
Outputs:
- p_factor: float32 [2, 4608, 8], replicated
- q_factor: float32 [2, 256, 8], replicated
- new_errors: bfloat16 [2, 1179648, 256], P(None, ('row', 'col'))
The draws below stay inside these ranges and needn't reach their ends.
All inputs are finite; a program needn't handle non-finite values.
Results may differ from the reference program's by a relative error of at most 0.001.
Values sent between devices are 32-bit elements; how exact they have to be, the bound alone decides.
A program may use at most 128 MiB of HBM per device.

```python
import math
import jax
import jax.numpy as jnp
from jax import lax

C_IN = 512
C_OUT = 256
RANK = 8
LAYERS = 2
SIDE = 24
IMG_DEV = 2
KDIM = 4608
IMAGES = 512
DEVICES = 256


def draw_errors(key, part):
    key = jax.random.fold_in(key, 11)
    k_common, k_cols, k_noise = jax.random.split(key, 3)
    common = 0.4 * jnp.clip(jax.random.normal(k_common, (LAYERS, KDIM, C_OUT), jnp.float32), -4.0, 4.0)
    col_scale = jnp.exp(jax.random.uniform(k_cols, (LAYERS, 1, C_OUT), jnp.float32, math.log(0.3), math.log(3.0)))
    common = common * col_scale
    noise = 0.5 * jnp.clip(jax.random.normal(k_noise, (LAYERS, DEVICES, KDIM, C_OUT), jnp.float32), -6.0, 6.0)
    total = noise + common[:, None, :, :]
    return total.reshape(LAYERS, DEVICES * KDIM, C_OUT).astype(jnp.bfloat16)


def block_scale(stream_key, dims, cuts, smallest, high):
    def one(axis_at, blocks):
        steps = jax.random.uniform(jax.random.fold_in(jax.random.fold_in(stream_key, 6), axis_at), (blocks,), jnp.float32, smallest / len(cuts), high / len(cuts))
        return jnp.repeat(jnp.exp(steps), dims[axis_at] // blocks).reshape((-1,) + (1,) * (len(dims) - axis_at - 1))

    gain = one(*cuts[0])
    for cut in cuts[1:]:
        gain = gain * one(*cut)
    return gain


def bell_draw(stream_key, extent, scale, most, cuts=(), kind=jnp.bfloat16):
    loudness = block_scale(stream_key, extent, cuts, -0.22, 0.18) if cuts else 1.0
    drawn = jax.random.normal(stream_key, extent, jnp.float32) * scale * loudness
    return jnp.minimum(jnp.maximum(drawn, -most), most).astype(kind)


def setup_inputs(seed: int = 0) -> dict:
    keys = jax.random.split(jax.random.key(seed), 5)
    return {
        "activations": bell_draw(keys[0], (LAYERS, IMAGES, SIDE, SIDE, C_IN), 1.0, 6.0, ((1, 256),)),
        "out_grads": bell_draw(keys[1], (LAYERS, IMAGES, SIDE, SIDE, C_OUT), 1.0, 6.0, ((1, 256),)),
        "errors": draw_errors(jax.random.fold_in(keys[4], 71), 0),
        "q_start": bell_draw(keys[3], (LAYERS, C_OUT, RANK), 1.0, 6.0, (), jnp.float32),
    }


grad_scale = 0.03125
epsilon = 1e-06

def local_grad(inputs, upstream):
    side_len = inputs.shape[1]
    padded = jnp.pad(inputs, ((0, 0), (1, 1), (1, 1), (0, 0)))
    flat_up = upstream.reshape(-1, upstream.shape[-1])
    blocks = []
    for tap_row in range(3):
        for tap_col in range(3):
            window = padded[:, tap_row:tap_row + side_len, tap_col:tap_col + side_len, :].reshape(-1, inputs.shape[-1])
            blocks.append(lax.dot_general(window, flat_up, (((0,), (0,)), ((), ())), preferred_element_type=jnp.float32))
    return jnp.concatenate(blocks, axis=0) * grad_scale

def orthonormal(factors):
    columns = []
    for index in range(factors.shape[-1]):
        column = factors[..., index]
        for earlier in columns:
            column = column - lax.optimization_barrier(jnp.sum(earlier * column, axis=-1, keepdims=True)) * earlier
        column = column / jnp.sqrt(lax.optimization_barrier(jnp.sum(column * column, axis=-1, keepdims=True)) + epsilon)
        columns.append(column)
    return jnp.stack(columns, axis=-1)

def reference(activations, out_grads, errors, q_start):
    highest = lax.Precision.HIGHEST
    p_list = []
    q_list = []
    e_list = []
    for layer_idx in range(LAYERS):
        acts = activations[layer_idx].reshape(DEVICES, IMG_DEV, SIDE, SIDE, C_IN)
        upstream = out_grads[layer_idx].reshape(DEVICES, IMG_DEV, SIDE, SIDE, C_OUT)
        memory = errors[layer_idx].reshape(DEVICES, KDIM, C_OUT)
        merged = lax.map(lambda items: local_grad(items[0], items[1]) + items[2].astype(jnp.float32), (acts, upstream, memory))
        p_mean = jnp.einsum('dkc,cr->kr', merged, q_start[layer_idx], precision=highest) / DEVICES
        p_hat = orthonormal(p_mean[None])[0]
        q_mean = jnp.einsum('dkc,kr->cr', merged, p_hat, precision=highest) / DEVICES
        approx = jnp.dot(p_hat, q_mean.T, precision=highest)
        new_err = (merged - approx[None]).astype(jnp.bfloat16).reshape(DEVICES * KDIM, C_OUT)
        p_list.append(p_hat)
        q_list.append(q_mean)
        e_list.append(new_err)
    return (jnp.stack(p_list), jnp.stack(q_list), jnp.stack(e_list))
```

```python
import functools
import jax
import jax.numpy as jnp
from jax import lax
from jax.experimental import pallas as pl
from jax.experimental.pallas import tpu as pltpu
from jax.sharding import PartitionSpec as P

grad_scale = 0.03125
epsilon = 1e-06
f32 = jnp.float32
bf16 = jnp.bfloat16
MESH = pl.DeviceIdType.MESH

LAYERS, SIDE, PIX, CIN, COUT, RANK, KDIM = 2, 24, 1152, 512, 256, 8, 4608
IMG = SIDE * SIDE
TILES = KDIM // 128
NXY, NZ = 16, 8


def halves(v):
    hi = v.astype(bf16).astype(f32)
    return jnp.concatenate([hi, v - hi], axis=0).astype(bf16)


def dot_nt(a, b):
    return lax.dot_general(a, b, (((1,), (1,)), ((), ())), preferred_element_type=f32)


def dot(a, b):
    return jnp.dot(a, b, preferred_element_type=f32)


def place(shape, axis):
    pix = lax.broadcasted_iota(jnp.int32, shape, axis).astype(f32)
    line = jnp.floor((pix + 0.5) * (1.0 / SIDE))
    col = pix - line * SIDE
    row = line - jnp.floor((line + 0.5) * (1.0 / SIDE)) * SIDE
    return col, row


def orthonormal(layers):
    rank = lax.broadcasted_iota(jnp.int32, (1, RANK, 1), 1)
    layers = list(layers)
    scales = [jnp.zeros((1, RANK, 1), f32) for _ in layers]
    for j in range(RANK):
        for k, c in enumerate(layers):
            cj = c[:, j : j + 1, :]
            prod = c[:TILES] * cj[:TILES]
            dots = jnp.sum(jnp.sum(prod, axis=0, keepdims=True), axis=2, keepdims=True)
            square = dots[:, j : j + 1, :] + epsilon
            scales[k] = jnp.where(rank == j, 1.0 / jnp.sqrt(square), scales[k])
            if j < RANK - 1:
                layers[k] = c - jnp.where(rank > j, dots / square, 0.0) * cj
    return [c * scale for c, scale in zip(layers, scales)]


def far_first(offsets, sizes):
    return sorted(offsets, key=lambda d: -sum(min(i, n - i) for i, n in zip(d, sizes)))


NEAR = far_first([(i, j) for i in range(4) for j in range(4) if i or j], (4, 4))
FAR = far_first([(k,) for k in range(1, NZ)], (NZ,))
PIECES = 1
PROWS = KDIM // PIECES
FIRST, AT_RS, AT_Z = 3, 6, 12


def main_kernel(
    x_hbm, g_hbm, e_hbm, q0_hbm,
    merged, amat, ph_out, q_out,
    xv, gv, ev, qv, xt, gpad, mhi, mlo,
    ws, pbuf, prx, psum, rs_rx, zbuf, pown, pfull, pex, ph, rowop,
    mrx, qx, qz, qf,
    load_sem, send_sem, recv_sem, piece_sem, line_sem,
):
    z = lax.axis_index("row")
    col = lax.axis_index("col")
    core = lax.rem(col, 2)
    chip = col // 2
    other = 1 - core
    partner = (z, chip * 2 + other)
    cx, cy = chip // 4, lax.rem(chip, 4)
    chips = [lax.rem(cx + i, 4) * 4 + lax.rem(cy + j, 4) for i, j in NEAR]
    near = [(z, t * 2 + 1) for t in chips]
    near_0 = [(z, t * 2) for t in chips]
    far = [(lax.rem(z + k, NZ), col) for (k,) in FAR]

    def layer_of(k):
        return other + k * (core - other)

    def load(what, k):
        layer = layer_of(k)
        if what == "q":
            return pltpu.make_async_copy(q0_hbm, qv, load_sem.at[0])
        if what == "g":
            return pltpu.make_async_copy(g_hbm.at[layer], gv.at[layer], load_sem.at[1 + k])
        if what == "x":
            return pltpu.make_async_copy(x_hbm.at[layer], xv.at[layer], load_sem.at[3 + k])
        rows = pl.ds(what * PROWS, PROWS)
        return pltpu.make_async_copy(e_hbm.at[layer, rows], ev.at[layer, rows], load_sem.at[5 + 2 * what + k])

    load("q", 0).start()
    for what, k in [("g", 0), ("g", 1)] + [(what, k) for k in range(2) for what in ("x",) + tuple(range(PIECES))]:
        load(what, k).start()

    barrier = pltpu.get_barrier_semaphore()
    for device in [partner] + near:
        pl.semaphore_signal(barrier, inc=1, device_id=device, device_id_type=MESH)

    @pl.when(core == 1)
    def _():
        for device in near_0 + far:
            pl.semaphore_signal(barrier, inc=1, device_id=device, device_id_type=MESH)

    def send(src, dst, k, device, recv=None):
        pltpu.make_async_remote_copy(
            src_ref=src, dst_ref=dst, send_sem=send_sem.at[k], recv_sem=recv_sem.at[k if recv is None else recv],
            device_id=device, device_id_type=MESH,
        ).start()

    def arrived(ref, k):
        pltpu.make_async_copy(ref, ref, recv_sem.at[k]).wait()

    def sent(ref, k):
        pltpu.make_async_copy(ref, ref, send_sem.at[k]).wait()

    xcol, xrow = place((RANK, PIX), 1)

    load("q", 0).wait()

    @pl.loop(0, 2)
    def _(k):
        layer = layer_of(k)
        q = halves(qv[layer])
        load("g", k).wait()
        u = dot_nt(q, gv[layer])
        u = u[:RANK] + u[RANK:]
        parts = []
        for a in range(3):
            for b in range(3):
                shift = SIDE * (a - 1) + (b - 1)
                part = pltpu.roll(u, shift % PIX, 1) if shift else u
                ok = None
                for tap, pos in ((a, xrow), (b, xcol)):
                    if tap != 1:
                        here = pos < SIDE - 1.5 if tap == 0 else pos > 0.5
                        ok = here if ok is None else jnp.logical_and(ok, here)
                parts.append(part if ok is None else jnp.where(ok, part, 0.0))
        ws[k] = halves(jnp.concatenate(parts, axis=0))

    @pl.loop(0, 2)
    def _(k):
        layer = layer_of(k)
        q = halves(qv[layer])
        load("x", k).wait()
        pg = dot(ws[k], xv[layer])
        pg = (pg[: 9 * RANK] + pg[9 * RANK :]) * grad_scale
        for n in range(PIECES):
            load(n, k).wait()
            pe = dot_nt(q, ev[layer, n * PROWS : (n + 1) * PROWS])
            pe = pe[:RANK] + pe[RANK:]
            for i in range(PROWS // 128):
                t = n * (PROWS // 128) + i
                tap, part = divmod(t, 4)
                tile = pe[:, 128 * i : 128 * i + 128] + pg[RANK * tap : RANK * tap + RANK, 128 * part : 128 * part + 128]
                for r in range(4):
                    pbuf[k, r * 4 + t // 9, t % 9] = tile[2 * r : 2 * r + 2]

        @pl.when(k == 0)
        def _():
            pl.semaphore_wait(barrier, 16 + 22 * core)
            send(pbuf.at[0], prx, 0, partner)

    arrived(prx, 0)
    psum[...] = pbuf[1] + prx[...]

    for t, device in zip(chips, near):
        send(psum.at[t], rs_rx.at[core, chip], 1, device, 10 + core)

    @pl.when(core == 0)
    def _():
        send(psum.at[chip], rs_rx.at[0, chip], 1, partner, 10)

    @pl.when(core == 1)
    def _():
        rs_rx[1, chip] = psum[chip]

    gpad[:, :, :SIDE] = jnp.zeros((3, 2, SIDE, COUT), f32)
    gpad[:, :, SIDE + IMG :] = jnp.zeros((3, 2, SIDE, COUT), f32)

    def prepare(layer):
        xt[...] = jnp.transpose(xv[layer])
        gcol, _ = place((PIX, COUT), 0)
        g = gv[layer].astype(f32)
        for b in range(3):
            if b == 1:
                part = g
            elif b == 0:
                part = jnp.where(gcol < SIDE - 1.5, pltpu.roll(g, PIX - 1, 0), 0.0)
            else:
                part = jnp.where(gcol > 0.5, pltpu.roll(g, 1, 0), 0.0)
            for i in range(2):
                gpad[b, i, SIDE : SIDE + IMG] = part[i * IMG : (i + 1) * IMG]

    def give(tap):
        rows = pl.ds(pl.multiple_of(tap * CIN, CIN), CIN)
        pltpu.make_async_remote_copy(
            src_ref=merged.at[other, rows], dst_ref=mrx.at[rows], send_sem=send_sem.at[9],
            recv_sem=piece_sem.at[tap], device_id=partner, device_id_type=MESH,
        ).start()

    @pl.loop(0, 18)
    def _(step):
        k = step // 9
        tap = step - 9 * k
        layer = layer_of(k)

        @pl.when(tap == 0)
        def _():
            prepare(layer)

        b = lax.rem(tap, 3)
        start = pl.multiple_of(2 * SIDE - SIDE * (tap // 3), 8)
        window = jnp.concatenate([gpad[b, i, pl.ds(start, IMG)] for i in range(2)], axis=0).astype(bf16)
        rows = pl.ds(pl.multiple_of(tap * CIN, CIN), CIN)
        total = dot(xt[...], window) * grad_scale + ev[layer, rows].astype(f32)
        merged[layer, rows] = total

        @pl.when(jnp.logical_or(step < FIRST, jnp.logical_and(step >= AT_RS, step < 8)))
        def _():
            give(tap)

        @pl.when(k == 1)
        def _():
            pltpu.make_async_copy(mrx.at[rows], mrx.at[rows], piece_sem.at[tap]).wait()
            both = total + mrx[rows]
            hi = both.astype(bf16)
            mhi[rows] = hi
            mlo[rows] = (both - hi.astype(f32)).astype(bf16)

        @pl.when(jnp.logical_and(step == AT_RS - 1, core == 1))
        def _():
            arrived(rs_rx.at[0], 10)
            arrived(rs_rx.at[1, pl.ds(0, 15)], 11)
            for i in range(LAYERS):
                part = rs_rx[i, 0]
                for n in range(1, NXY):
                    part = part + rs_rx[i, n]
                zbuf[z, i] = part

            for device in far:
                send(zbuf.at[z], zbuf.at[z], 2, device)

        @pl.when(step == AT_RS - 1)
        def _():
            for n in range(FIRST, AT_RS):
                give(n)

        @pl.when(jnp.logical_and(step == AT_Z - 1, core == 1))
        def _():
            arrived(zbuf.at[pl.ds(0, 7)], 2)
            for i in range(LAYERS):
                part = zbuf[0, i]
                for n in range(1, NZ):
                    part = part + zbuf[n, i]
                part = part * (1.0 / 256.0)
                if i == 0:
                    pown[...] = part
                else:
                    pfull[chip] = part

            def spread(src, k, device):
                pltpu.make_async_remote_copy(
                    src_ref=src, dst_ref=pfull.at[chip], send_sem=send_sem.at[k], recv_sem=line_sem.at[cy],
                    device_id=device, device_id_type=MESH,
                ).start()

            for device_0, device in zip(near_0, near):
                spread(pown, 10, device_0)
                spread(pfull.at[chip], 3, device)
            spread(pown, 10, partner)

        @pl.when(step == AT_Z - 1)
        def _():
            give(8)

    def line(n, total):
        y = lax.rem(cy + n + jnp.where(n == 2, 1, 0) - jnp.where(n == 3, 1, 0), 4)
        here = line_sem.at[y]

        mine = jnp.logical_and(n == 0, core == 1)

        @pl.when(mine)
        def _():
            pltpu.make_async_copy(pfull.at[pl.ds(0, 3)], pfull.at[pl.ds(0, 3)], here).wait()

        @pl.when(jnp.logical_not(mine))
        def _():
            pltpu.make_async_copy(pfull.at[pl.ds(0, 4)], pfull.at[pl.ds(0, 4)], here).wait()

        tiles = pl.ds(9 * y, 9)
        for r in range(4):
            pex[tiles, 2 * r : 2 * r + 2, :] = pfull[4 * r + y]
        left = halves(jnp.concatenate([pex[9 * y + i] for i in range(9)], axis=1))
        rows = pl.ds(pl.multiple_of(y * (KDIM // 4), KDIM // 4), KDIM // 4)
        return total + dot(left, mhi[rows]) + dot(left, mlo[rows])

    right = lax.fori_loop(0, 4, line, jnp.zeros((2 * RANK, COUT), f32))
    qx[core, chip] = right[:RANK] + right[RANK:]
    for device in near:
        send(qx.at[core, chip], qx.at[core, chip], 6, device, 12 + core)

    @pl.when(core == 0)
    def _():
        send(qx.at[0, chip], qx.at[0, chip], 6, partner, 12)

    unit = lax.broadcasted_iota(jnp.int32, (1, RANK, 128), 1) == lax.broadcasted_iota(jnp.int32, (1, RANK, 128), 2)
    unit = jnp.where(unit, 1.0, 0.0).astype(f32)
    (done,) = orthonormal([jnp.concatenate([pex[...], unit], axis=0)])
    ph[core] = done[:TILES]
    send(ph.at[core], ph.at[core], 4, partner)
    for s in range(RANK):
        rowop[core, s] = jnp.broadcast_to(done[TILES][:, s : s + 1], (RANK, COUT))
    send(rowop.at[core], rowop.at[core], 5, partner)

    def for_tail(layer):
        for t in range(0, TILES, 4):
            v = jnp.concatenate([ph[layer, t + k] for k in range(4)], axis=1)
            ph_out[layer, :, 128 * t : 128 * t + 512] = v
            hi = v.astype(bf16).astype(f32)
            both = jnp.concatenate([hi, v - hi, hi, jnp.zeros_like(hi)], axis=0)
            amat[layer, 128 * t : 128 * t + 512] = jnp.transpose(both).astype(bf16)

    for_tail(core)
    @pl.when(core == 1)
    def _():
        arrived(qx.at[0], 12)
        arrived(qx.at[1, pl.ds(0, 15)], 13)
        for i in range(LAYERS):
            part = qx[i, 0]
            for n in range(1, NXY):
                part = part + qx[i, n]
            qz[z, i] = part
        for device in far:
            send(qz.at[z], qz.at[z], 7, device)

    arrived(ph.at[0], 4)
    arrived(rowop.at[0], 5)
    for_tail(other)
    sent(pbuf.at[0], 0)
    sent(ph.at[0], 4)
    sent(rowop.at[0], 5)
    sent(merged.at[0], 9)

    @pl.when(core == 0)
    def _():
        sent(psum, 1)
        sent(qx.at[0], 6)
        arrived(qf, 8)

    @pl.when(core == 1)
    def _():
        sent(psum.at[pl.ds(0, 15)], 1)
        sent(zbuf.at[pl.ds(0, 7)], 2)
        sent(pfull.at[pl.ds(0, 15)], 3)
        sent(pfull, 10)
        sent(qx.at[0, pl.ds(0, 15)], 6)
        sent(qz.at[pl.ds(0, 7)], 7)
        arrived(qz.at[pl.ds(0, 7)], 7)
        for i in range(LAYERS):
            part = qz[0, i]
            for n in range(1, NZ):
                part = part + qz[n, i]
            part = part * (1.0 / 256.0)
            right = rowop[i, 0] * part[0:1]
            for s in range(1, RANK):
                right = right + rowop[i, s] * part[s : s + 1]
            qf[i] = right
        send(qf, qf, 8, partner)
        sent(qf, 8)

    q_out[...] = qf[...]


CHUNK = 256


def tail_kernel(merged, amat, ph, q, p_hbm, q_hbm, e_hbm, stage, sem):
    outs = [pltpu.make_async_copy(ph, p_hbm, sem.at[0]), pltpu.make_async_copy(q, q_hbm, sem.at[1])]
    for copy in outs:
        copy.start()
    for layer in range(LAYERS):
        qh = q[layer]
        hi = qh.astype(bf16).astype(f32)
        right = jnp.concatenate([hi, hi, qh - hi, jnp.zeros_like(hi)], axis=0).astype(bf16)
        for c in range(KDIM // CHUNK):
            rows = slice(c * CHUNK, (c + 1) * CHUNK)
            low = dot(amat[layer, rows], right)
            stage[layer, rows] = (merged[layer, rows] - low).astype(bf16)
            copy = pltpu.make_async_copy(stage.at[layer, rows], e_hbm.at[layer, rows], sem.at[2 + layer * (KDIM // CHUNK) + c])
            copy.start()
            outs.append(copy)
    for copy in outs:
        copy.wait()


def body(activations, out_grads, errors, q_start):
    x = activations.reshape(LAYERS, PIX, CIN)
    g = out_grads.reshape(LAYERS, PIX, COUT)
    q0 = jnp.transpose(q_start, (0, 2, 1))
    x, g, errors, q0 = (pltpu.with_memory_space_constraint(a, pltpu.HBM) for a in (x, g, errors, q0))
    hbm = pl.BlockSpec(memory_space=pltpu.HBM)
    vmem = pl.BlockSpec(memory_space=pltpu.VMEM)
    V = pltpu.VMEM
    chunks = (9, 2, 128)
    merged, amat, ph, q = pl.pallas_call(
        main_kernel,
        out_shape=[
            V((LAYERS, KDIM, COUT), f32),
            V((LAYERS, KDIM, 4 * RANK), bf16),
            V((LAYERS, RANK, KDIM), f32),
            V((LAYERS, RANK, COUT), f32),
        ],
        in_specs=[hbm] * 4,
        out_specs=[vmem] * 4,
        scratch_shapes=[
            V((LAYERS, PIX, CIN), bf16),
            V((LAYERS, PIX, COUT), bf16),
            V((LAYERS, KDIM, COUT), bf16),
            V((LAYERS, RANK, COUT), f32),
            V((CIN, PIX), bf16),
            V((3, 2, IMG + 2 * SIDE, COUT), f32),
            V((KDIM, COUT), bf16),
            V((KDIM, COUT), bf16),
            V((2, 2 * 9 * RANK, PIX), bf16),
            V((2, NXY) + chunks, f32),
            V((NXY,) + chunks, f32),
            V((NXY,) + chunks, f32),
            V((LAYERS, NXY) + chunks, f32),
            V((NZ, LAYERS) + chunks, f32),
            V(chunks, f32),
            V((NXY,) + chunks, f32),
            V((TILES, RANK, 128), f32),
            V((LAYERS, TILES, RANK, 128), f32),
            V((LAYERS, RANK, RANK, COUT), f32),
            V((KDIM, COUT), f32),
            V((LAYERS, NXY, RANK, COUT), f32),
            V((NZ, LAYERS, RANK, COUT), f32),
            V((LAYERS, RANK, COUT), f32),
            pltpu.SemaphoreType.DMA((11,)),
            pltpu.SemaphoreType.DMA((11,)),
            pltpu.SemaphoreType.DMA((14,)),
            pltpu.SemaphoreType.DMA((9,)),
            pltpu.SemaphoreType.DMA((4,)),
        ],
        compiler_params=pltpu.CompilerParams(
            collective_id=0, has_side_effects=True, vmem_limit_bytes=32 << 20
        ),
        cost_estimate=pl.CostEstimate(flops=2 * 2 * KDIM * PIX * COUT, bytes_accessed=9 << 20, transcendentals=0),
        name="factors",
    )(x, g, errors, q0)
    p_t, q_t, new_errors = pl.pallas_call(
        tail_kernel,
        out_shape=[
            jax.ShapeDtypeStruct((LAYERS, RANK, KDIM), f32),
            jax.ShapeDtypeStruct((LAYERS, RANK, COUT), f32),
            jax.ShapeDtypeStruct((LAYERS, KDIM, COUT), bf16),
        ],
        in_specs=[vmem] * 4,
        out_specs=[hbm] * 3,
        scratch_shapes=[V((LAYERS, KDIM, COUT), bf16), pltpu.SemaphoreType.DMA((2 + 2 * (KDIM // CHUNK),))],
        compiler_params=pltpu.CompilerParams(vmem_limit_bytes=32 << 20),
        cost_estimate=pl.CostEstimate(flops=2 * 2 * KDIM * 32 * COUT, bytes_accessed=5 << 20, transcendentals=0),
        name="memory_update",
    )(merged, amat, ph, q)
    return jnp.transpose(p_t, (0, 2, 1)), jnp.transpose(q_t, (0, 2, 1)), new_errors


def solution(mesh):
    placed = (
        P(None, ("row", "col"), None, None, None),
        P(None, ("row", "col"), None, None, None),
        P(None, ("row", "col"), None),
        P(),
    )
    return jax.shard_map(
        body,
        mesh=mesh,
        in_specs=placed,
        out_specs=(P(), P(), P(None, ("row", "col"), None)),
        check_vma=False,
    )
```

```python
import functools
import jax
import jax.numpy as jnp
from jax import lax
from jax.experimental import pallas as pl
from jax.experimental.pallas import tpu as pltpu
from jax.sharding import PartitionSpec as P

grad_scale = 0.03125
epsilon = 1e-06
f32 = jnp.float32
bf16 = jnp.bfloat16
MESH = pl.DeviceIdType.MESH

LAYERS, SIDE, PIX, CIN, COUT, RANK, KDIM = 2, 24, 1152, 512, 256, 8, 4608
IMG = SIDE * SIDE
TILES = KDIM // 128
NXY, NZ = 16, 8


def halves(v):
    hi = v.astype(bf16).astype(f32)
    return jnp.concatenate([hi, v - hi], axis=0).astype(bf16)


def dot_nt(a, b):
    return lax.dot_general(a, b, (((1,), (1,)), ((), ())), preferred_element_type=f32)


def dot(a, b):
    return jnp.dot(a, b, preferred_element_type=f32)


def place(shape, axis):
    pix = lax.broadcasted_iota(jnp.int32, shape, axis).astype(f32)
    line = jnp.floor((pix + 0.5) * (1.0 / SIDE))
    col = pix - line * SIDE
    row = line - jnp.floor((line + 0.5) * (1.0 / SIDE)) * SIDE
    return col, row


def orthonormal(layers):
    rank = lax.broadcasted_iota(jnp.int32, (1, RANK, 1), 1)
    layers = list(layers)
    scales = [jnp.zeros((1, RANK, 1), f32) for _ in layers]
    for j in range(RANK):
        for k, c in enumerate(layers):
            cj = c[:, j : j + 1, :]
            prod = c[:TILES] * cj[:TILES]
            dots = jnp.sum(jnp.sum(prod, axis=0, keepdims=True), axis=2, keepdims=True)
            square = dots[:, j : j + 1, :] + epsilon
            scales[k] = jnp.where(rank == j, 1.0 / jnp.sqrt(square), scales[k])
            if j < RANK - 1:
                layers[k] = c - jnp.where(rank > j, dots / square, 0.0) * cj
    return [c * scale for c, scale in zip(layers, scales)]


def far_first(offsets, sizes):
    return sorted(offsets, key=lambda d: -sum(min(i, n - i) for i, n in zip(d, sizes)))


NEAR = far_first([(i, j) for i in range(4) for j in range(4) if i or j], (4, 4))
FAR = far_first([(k,) for k in range(1, NZ)], (NZ,))
PIECES = 1
PROWS = KDIM // PIECES
AT_RS, AT_Z = 2, 4


def main_kernel(
    x_hbm, g_hbm, e_hbm, q0_hbm,
    merged, amat, ph_out, q_out,
    xv, gv, ev, qv, xt, gpad, mhi, mlo,
    ws, pbuf, prx, psum, rs_rx, zbuf, pown, pfull, pex, ph, rowop,
    mrx, qx, qz, qf,
    load_sem, send_sem, recv_sem, piece_sem, line_sem,
):
    z = lax.axis_index("row")
    col = lax.axis_index("col")
    core = lax.rem(col, 2)
    chip = col // 2
    other = 1 - core
    partner = (z, chip * 2 + other)
    cx, cy = chip // 4, lax.rem(chip, 4)
    chips = [lax.rem(cx + i, 4) * 4 + lax.rem(cy + j, 4) for i, j in NEAR]
    near = [(z, t * 2 + 1) for t in chips]
    near_0 = [(z, t * 2) for t in chips]
    far = [(lax.rem(z + k, NZ), col) for (k,) in FAR]

    def layer_of(k):
        return other + k * (core - other)

    def load(what, k):
        layer = layer_of(k)
        if what == "q":
            return pltpu.make_async_copy(q0_hbm, qv, load_sem.at[0])
        if what == "g":
            return pltpu.make_async_copy(g_hbm.at[layer], gv.at[layer], load_sem.at[1 + k])
        if what == "x":
            return pltpu.make_async_copy(x_hbm.at[layer], xv.at[layer], load_sem.at[3 + k])
        rows = pl.ds(what * PROWS, PROWS)
        return pltpu.make_async_copy(e_hbm.at[layer, rows], ev.at[layer, rows], load_sem.at[5 + 2 * what + k])

    load("q", 0).start()
    for what, k in [("g", 0), ("g", 1)] + [(what, k) for k in range(2) for what in ("x",) + tuple(range(PIECES))]:
        load(what, k).start()

    barrier = pltpu.get_barrier_semaphore()
    for device in [partner] + near:
        pl.semaphore_signal(barrier, inc=1, device_id=device, device_id_type=MESH)

    @pl.when(core == 1)
    def _():
        for device in near_0 + far:
            pl.semaphore_signal(barrier, inc=1, device_id=device, device_id_type=MESH)

    def send(src, dst, k, device, recv=None):
        pltpu.make_async_remote_copy(
            src_ref=src, dst_ref=dst, send_sem=send_sem.at[k], recv_sem=recv_sem.at[k if recv is None else recv],
            device_id=device, device_id_type=MESH,
        ).start()

    def arrived(ref, k):
        pltpu.make_async_copy(ref, ref, recv_sem.at[k]).wait()

    def sent(ref, k):
        pltpu.make_async_copy(ref, ref, send_sem.at[k]).wait()

    xcol, xrow = place((RANK, PIX), 1)

    load("q", 0).wait()

    @pl.loop(0, 2)
    def _(k):
        layer = layer_of(k)
        q = halves(qv[layer])
        load("g", k).wait()
        u = dot_nt(q, gv[layer])
        u = u[:RANK] + u[RANK:]
        parts = []
        for a in range(3):
            for b in range(3):
                shift = SIDE * (a - 1) + (b - 1)
                part = pltpu.roll(u, shift % PIX, 1) if shift else u
                ok = None
                for tap, pos in ((a, xrow), (b, xcol)):
                    if tap != 1:
                        here = pos < SIDE - 1.5 if tap == 0 else pos > 0.5
                        ok = here if ok is None else jnp.logical_and(ok, here)
                parts.append(part if ok is None else jnp.where(ok, part, 0.0))
        ws[k] = halves(jnp.concatenate(parts, axis=0))

    @pl.loop(0, 2)
    def _(k):
        layer = layer_of(k)
        q = halves(qv[layer])
        load("x", k).wait()
        pg = dot(ws[k], xv[layer])
        pg = (pg[: 9 * RANK] + pg[9 * RANK :]) * grad_scale
        for n in range(PIECES):
            load(n, k).wait()
            pe = dot_nt(q, ev[layer, n * PROWS : (n + 1) * PROWS])
            pe = pe[:RANK] + pe[RANK:]
            for i in range(PROWS // 128):
                t = n * (PROWS // 128) + i
                tap, part = divmod(t, 4)
                tile = pe[:, 128 * i : 128 * i + 128] + pg[RANK * tap : RANK * tap + RANK, 128 * part : 128 * part + 128]
                for r in range(4):
                    pbuf[k, r * 4 + t // 9, t % 9] = tile[2 * r : 2 * r + 2]

        @pl.when(k == 0)
        def _():
            pl.semaphore_wait(barrier, 16 + 22 * core)
            send(pbuf.at[0], prx, 0, partner)

    arrived(prx, 0)
    psum[...] = pbuf[1] + prx[...]

    for t, device in zip(chips, near):
        send(psum.at[t], rs_rx.at[core, chip], 1, device, 10 + core)

    @pl.when(core == 0)
    def _():
        send(psum.at[chip], rs_rx.at[0, chip], 1, partner, 10)

    @pl.when(core == 1)
    def _():
        rs_rx[1, chip] = psum[chip]

    gpad[:, :, :SIDE] = jnp.zeros((3, 2, SIDE, COUT), f32)
    gpad[:, :, SIDE + IMG :] = jnp.zeros((3, 2, SIDE, COUT), f32)

    def prepare(layer):
        xt[...] = jnp.transpose(xv[layer])
        gcol, _ = place((PIX, COUT), 0)
        g = gv[layer].astype(f32)
        for b in range(3):
            if b == 1:
                part = g
            elif b == 0:
                part = jnp.where(gcol < SIDE - 1.5, pltpu.roll(g, PIX - 1, 0), 0.0)
            else:
                part = jnp.where(gcol > 0.5, pltpu.roll(g, 1, 0), 0.0)
            for i in range(2):
                gpad[b, i, SIDE : SIDE + IMG] = part[i * IMG : (i + 1) * IMG]

    def give(tap):
        rows = pl.ds(pl.multiple_of(tap * CIN, CIN), CIN)
        pltpu.make_async_remote_copy(
            src_ref=merged.at[other, rows], dst_ref=mrx.at[rows], send_sem=send_sem.at[9],
            recv_sem=piece_sem.at[tap], device_id=partner, device_id_type=MESH,
        ).start()

    @pl.loop(0, 6)
    def _(step):
        k = step // 3
        a = step - 3 * k
        layer = layer_of(k)

        @pl.when(a == 0)
        def _():
            prepare(layer)

        start = pl.multiple_of(2 * SIDE - SIDE * a, 8)
        for b in range(3):
            window = jnp.concatenate([gpad[b, i, pl.ds(start, IMG)] for i in range(2)], axis=0).astype(bf16)
            rows = pl.ds(pl.multiple_of((3 * a + b) * CIN, CIN), CIN)
            merged[layer, rows] = dot(xt[...], window) * grad_scale + ev[layer, rows].astype(f32)

        @pl.when(step == 0)
        def _():
            for n in range(3):
                give(n)

        @pl.when(step == 2)
        def _():
            for n in range(6, 8):
                give(n)

        @pl.when(k == 1)
        def _():
            for b in range(3):
                rows = pl.ds(pl.multiple_of((3 * a + b) * CIN, CIN), CIN)
                pltpu.make_async_copy(mrx.at[rows], mrx.at[rows], piece_sem.at[3 * a + b]).wait()
                both = merged[layer, rows] + mrx[rows]
                hi = both.astype(bf16)
                mhi[rows] = hi
                mlo[rows] = (both - hi.astype(f32)).astype(bf16)

        @pl.when(jnp.logical_and(step == AT_RS - 1, core == 1))
        def _():
            arrived(rs_rx.at[0], 10)
            arrived(rs_rx.at[1, pl.ds(0, 15)], 11)
            for i in range(LAYERS):
                part = rs_rx[i, 0]
                for n in range(1, NXY):
                    part = part + rs_rx[i, n]
                zbuf[z, i] = part

            for device in far:
                send(zbuf.at[z], zbuf.at[z], 2, device)

        @pl.when(step == AT_RS - 1)
        def _():
            for n in range(3, 6):
                give(n)

        @pl.when(jnp.logical_and(step == AT_Z - 1, core == 1))
        def _():
            arrived(zbuf.at[pl.ds(0, 7)], 2)
            for i in range(LAYERS):
                part = zbuf[0, i]
                for n in range(1, NZ):
                    part = part + zbuf[n, i]
                part = part * (1.0 / 256.0)
                if i == 0:
                    pown[...] = part
                else:
                    pfull[chip] = part

            def spread(src, k, device):
                pltpu.make_async_remote_copy(
                    src_ref=src, dst_ref=pfull.at[chip], send_sem=send_sem.at[k], recv_sem=line_sem.at[cy],
                    device_id=device, device_id_type=MESH,
                ).start()

            for device_0, device in zip(near_0, near):
                spread(pown, 10, device_0)
                spread(pfull.at[chip], 3, device)
            spread(pown, 10, partner)

        @pl.when(step == AT_Z - 1)
        def _():
            give(8)

    def line(n, total):
        y = lax.rem(cy + n + jnp.where(n == 2, 1, 0) - jnp.where(n == 3, 1, 0), 4)
        here = line_sem.at[y]

        mine = jnp.logical_and(n == 0, core == 1)

        @pl.when(mine)
        def _():
            pltpu.make_async_copy(pfull.at[pl.ds(0, 3)], pfull.at[pl.ds(0, 3)], here).wait()

        @pl.when(jnp.logical_not(mine))
        def _():
            pltpu.make_async_copy(pfull.at[pl.ds(0, 4)], pfull.at[pl.ds(0, 4)], here).wait()

        tiles = pl.ds(9 * y, 9)
        for r in range(4):
            pex[tiles, 2 * r : 2 * r + 2, :] = pfull[4 * r + y]
        left = halves(jnp.concatenate([pex[9 * y + i] for i in range(9)], axis=1))
        rows = pl.ds(pl.multiple_of(y * (KDIM // 4), KDIM // 4), KDIM // 4)
        return total + dot(left, mhi[rows]) + dot(left, mlo[rows])

    right = lax.fori_loop(0, 4, line, jnp.zeros((2 * RANK, COUT), f32))
    qx[core, chip] = right[:RANK] + right[RANK:]
    for device in near:
        send(qx.at[core, chip], qx.at[core, chip], 6, device, 12 + core)

    @pl.when(core == 0)
    def _():
        send(qx.at[0, chip], qx.at[0, chip], 6, partner, 12)

    unit = lax.broadcasted_iota(jnp.int32, (1, RANK, 128), 1) == lax.broadcasted_iota(jnp.int32, (1, RANK, 128), 2)
    unit = jnp.where(unit, 1.0, 0.0).astype(f32)
    (done,) = orthonormal([jnp.concatenate([pex[...], unit], axis=0)])
    ph[core] = done[:TILES]
    send(ph.at[core], ph.at[core], 4, partner)
    for s in range(RANK):
        rowop[core, s] = jnp.broadcast_to(done[TILES][:, s : s + 1], (RANK, COUT))
    send(rowop.at[core], rowop.at[core], 5, partner)

    def for_tail(layer):
        for t in range(0, TILES, 4):
            v = jnp.concatenate([ph[layer, t + k] for k in range(4)], axis=1)
            ph_out[layer, :, 128 * t : 128 * t + 512] = v
            hi = v.astype(bf16).astype(f32)
            both = jnp.concatenate([hi, v - hi, hi, jnp.zeros_like(hi)], axis=0)
            amat[layer, 128 * t : 128 * t + 512] = jnp.transpose(both).astype(bf16)

    for_tail(core)
    @pl.when(core == 1)
    def _():
        arrived(qx.at[0], 12)
        arrived(qx.at[1, pl.ds(0, 15)], 13)
        for i in range(LAYERS):
            part = qx[i, 0]
            for n in range(1, NXY):
                part = part + qx[i, n]
            qz[z, i] = part
        for device in far:
            send(qz.at[z], qz.at[z], 7, device)

    arrived(ph.at[0], 4)
    arrived(rowop.at[0], 5)
    for_tail(other)
    sent(pbuf.at[0], 0)
    sent(ph.at[0], 4)
    sent(rowop.at[0], 5)
    sent(merged.at[0], 9)

    @pl.when(core == 0)
    def _():
        sent(psum, 1)
        sent(qx.at[0], 6)
        arrived(qf, 8)

    @pl.when(core == 1)
    def _():
        sent(psum.at[pl.ds(0, 15)], 1)
        sent(zbuf.at[pl.ds(0, 7)], 2)
        sent(pfull.at[pl.ds(0, 15)], 3)
        sent(pfull, 10)
        sent(qx.at[0, pl.ds(0, 15)], 6)
        sent(qz.at[pl.ds(0, 7)], 7)
        arrived(qz.at[pl.ds(0, 7)], 7)
        for i in range(LAYERS):
            part = qz[0, i]
            for n in range(1, NZ):
                part = part + qz[n, i]
            part = part * (1.0 / 256.0)
            right = rowop[i, 0] * part[0:1]
            for s in range(1, RANK):
                right = right + rowop[i, s] * part[s : s + 1]
            qf[i] = right
        send(qf, qf, 8, partner)
        sent(qf, 8)

    q_out[...] = qf[...]


CHUNK = 256


def tail_kernel(merged, amat, ph, q, p_hbm, q_hbm, e_hbm, stage, sem):
    outs = [pltpu.make_async_copy(ph, p_hbm, sem.at[0]), pltpu.make_async_copy(q, q_hbm, sem.at[1])]
    for copy in outs:
        copy.start()
    for layer in range(LAYERS):
        qh = q[layer]
        hi = qh.astype(bf16).astype(f32)
        right = jnp.concatenate([hi, hi, qh - hi, jnp.zeros_like(hi)], axis=0).astype(bf16)
        for c in range(KDIM // CHUNK):
            rows = slice(c * CHUNK, (c + 1) * CHUNK)
            low = dot(amat[layer, rows], right)
            stage[layer, rows] = (merged[layer, rows] - low).astype(bf16)
            copy = pltpu.make_async_copy(stage.at[layer, rows], e_hbm.at[layer, rows], sem.at[2 + layer * (KDIM // CHUNK) + c])
            copy.start()
            outs.append(copy)
    for copy in outs:
        copy.wait()


def body(activations, out_grads, errors, q_start):
    x = activations.reshape(LAYERS, PIX, CIN)
    g = out_grads.reshape(LAYERS, PIX, COUT)
    q0 = jnp.transpose(q_start, (0, 2, 1))
    x, g, errors, q0 = (pltpu.with_memory_space_constraint(a, pltpu.HBM) for a in (x, g, errors, q0))
    hbm = pl.BlockSpec(memory_space=pltpu.HBM)
    vmem = pl.BlockSpec(memory_space=pltpu.VMEM)
    V = pltpu.VMEM
    chunks = (9, 2, 128)
    merged, amat, ph, q = pl.pallas_call(
        main_kernel,
        out_shape=[
            V((LAYERS, KDIM, COUT), f32),
            V((LAYERS, KDIM, 4 * RANK), bf16),
            V((LAYERS, RANK, KDIM), f32),
            V((LAYERS, RANK, COUT), f32),
        ],
        in_specs=[hbm] * 4,
        out_specs=[vmem] * 4,
        scratch_shapes=[
            V((LAYERS, PIX, CIN), bf16),
            V((LAYERS, PIX, COUT), bf16),
            V((LAYERS, KDIM, COUT), bf16),
            V((LAYERS, RANK, COUT), f32),
            V((CIN, PIX), bf16),
            V((3, 2, IMG + 2 * SIDE, COUT), f32),
            V((KDIM, COUT), bf16),
            V((KDIM, COUT), bf16),
            V((2, 2 * 9 * RANK, PIX), bf16),
            V((2, NXY) + chunks, f32),
            V((NXY,) + chunks, f32),
            V((NXY,) + chunks, f32),
            V((LAYERS, NXY) + chunks, f32),
            V((NZ, LAYERS) + chunks, f32),
            V(chunks, f32),
            V((NXY,) + chunks, f32),
            V((TILES, RANK, 128), f32),
            V((LAYERS, TILES, RANK, 128), f32),
            V((LAYERS, RANK, RANK, COUT), f32),
            V((KDIM, COUT), f32),
            V((LAYERS, NXY, RANK, COUT), f32),
            V((NZ, LAYERS, RANK, COUT), f32),
            V((LAYERS, RANK, COUT), f32),
            pltpu.SemaphoreType.DMA((11,)),
            pltpu.SemaphoreType.DMA((11,)),
            pltpu.SemaphoreType.DMA((14,)),
            pltpu.SemaphoreType.DMA((9,)),
            pltpu.SemaphoreType.DMA((4,)),
        ],
        compiler_params=pltpu.CompilerParams(
            collective_id=0, has_side_effects=True, vmem_limit_bytes=32 << 20
        ),
        cost_estimate=pl.CostEstimate(flops=2 * 2 * KDIM * PIX * COUT, bytes_accessed=9 << 20, transcendentals=0),
        name="factors",
    )(x, g, errors, q0)
    p_t, q_t, new_errors = pl.pallas_call(
        tail_kernel,
        out_shape=[
            jax.ShapeDtypeStruct((LAYERS, RANK, KDIM), f32),
            jax.ShapeDtypeStruct((LAYERS, RANK, COUT), f32),
            jax.ShapeDtypeStruct((LAYERS, KDIM, COUT), bf16),
        ],
        in_specs=[vmem] * 4,
        out_specs=[hbm] * 3,
        scratch_shapes=[V((LAYERS, KDIM, COUT), bf16), pltpu.SemaphoreType.DMA((2 + 2 * (KDIM // CHUNK),))],
        compiler_params=pltpu.CompilerParams(vmem_limit_bytes=32 << 20),
        cost_estimate=pl.CostEstimate(flops=2 * 2 * KDIM * 32 * COUT, bytes_accessed=5 << 20, transcendentals=0),
        name="memory_update",
    )(merged, amat, ph, q)
    return jnp.transpose(p_t, (0, 2, 1)), jnp.transpose(q_t, (0, 2, 1)), new_errors


def solution(mesh):
    placed = (
        P(None, ("row", "col"), None, None, None),
        P(None, ("row", "col"), None, None, None),
        P(None, ("row", "col"), None),
        P(),
    )
    return jax.shard_map(
        body,
        mesh=mesh,
        in_specs=placed,
        out_specs=(P(), P(), P(None, ("row", "col"), None)),
        check_vma=False,
    )
```

```python
import functools
import jax
import jax.numpy as jnp
from jax import lax
from jax.experimental import pallas as pl
from jax.experimental.pallas import tpu as pltpu
from jax.sharding import PartitionSpec as P

grad_scale = 0.03125
epsilon = 1e-06
f32 = jnp.float32
bf16 = jnp.bfloat16
MESH = pl.DeviceIdType.MESH

LAYERS, SIDE, PIX, CIN, COUT, RANK, KDIM = 2, 24, 1152, 512, 256, 8, 4608
IMG = SIDE * SIDE
TILES = KDIM // 128
NXY, NZ = 16, 8


def halves(v):
    hi = v.astype(bf16).astype(f32)
    return jnp.concatenate([hi, v - hi], axis=0).astype(bf16)


def dot_nt(a, b):
    return lax.dot_general(a, b, (((1,), (1,)), ((), ())), preferred_element_type=f32)


def dot(a, b):
    return jnp.dot(a, b, preferred_element_type=f32)


def place(shape, axis):
    pix = lax.broadcasted_iota(jnp.int32, shape, axis).astype(f32)
    line = jnp.floor((pix + 0.5) * (1.0 / SIDE))
    col = pix - line * SIDE
    row = line - jnp.floor((line + 0.5) * (1.0 / SIDE)) * SIDE
    return col, row


def orthonormal(layers):
    rank = lax.broadcasted_iota(jnp.int32, (1, RANK, 1), 1)
    layers = list(layers)
    scales = [jnp.zeros((1, RANK, 1), f32) for _ in layers]
    for j in range(RANK):
        for k, c in enumerate(layers):
            cj = c[:, j : j + 1, :]
            prod = c[:TILES] * cj[:TILES]
            dots = jnp.sum(jnp.sum(prod, axis=0, keepdims=True), axis=2, keepdims=True)
            square = dots[:, j : j + 1, :] + epsilon
            scales[k] = jnp.where(rank == j, 1.0 / jnp.sqrt(square), scales[k])
            if j < RANK - 1:
                layers[k] = c - jnp.where(rank > j, dots / square, 0.0) * cj
    return [c * scale for c, scale in zip(layers, scales)]


def far_first(offsets, sizes):
    return sorted(offsets, key=lambda d: -sum(min(i, n - i) for i, n in zip(d, sizes)))


NEAR = far_first([(i, j) for i in range(4) for j in range(4) if i or j], (4, 4))
FAR = far_first([(k,) for k in range(1, NZ)], (NZ,))
PIECES = 1
PROWS = KDIM // PIECES
AT_RS, AT_Z = 2, 4


def main_kernel(
    x_hbm, g_hbm, e_hbm, q0_hbm,
    merged, amat, ph_out, q_out,
    xv, gv, ev, qv, xt, gpad, mhi, mlo,
    ws, pbuf, prx, psum, rs_rx, zbuf, pown, pfull, pex, ph, rowop,
    mrx, qx, qz,
    load_sem, send_sem, recv_sem, piece_sem, line_sem,
):
    z = lax.axis_index("row")
    col = lax.axis_index("col")
    core = lax.rem(col, 2)
    chip = col // 2
    other = 1 - core
    partner = (z, chip * 2 + other)
    cx, cy = chip // 4, lax.rem(chip, 4)
    chips = [lax.rem(cx + i, 4) * 4 + lax.rem(cy + j, 4) for i, j in NEAR]
    near = [(z, t * 2 + 1) for t in chips]
    near_0 = [(z, t * 2) for t in chips]
    far = [(lax.rem(z + k, NZ), col) for (k,) in FAR]

    def layer_of(k):
        return other + k * (core - other)

    def load(what, k):
        layer = layer_of(k)
        if what == "q":
            return pltpu.make_async_copy(q0_hbm, qv, load_sem.at[0])
        if what == "g":
            return pltpu.make_async_copy(g_hbm.at[layer], gv.at[layer], load_sem.at[1 + k])
        if what == "x":
            return pltpu.make_async_copy(x_hbm.at[layer], xv.at[layer], load_sem.at[3 + k])
        rows = pl.ds(what * PROWS, PROWS)
        return pltpu.make_async_copy(e_hbm.at[layer, rows], ev.at[layer, rows], load_sem.at[5 + 2 * what + k])

    load("q", 0).start()
    for what, k in [("g", 0), ("g", 1)] + [(what, k) for k in range(2) for what in ("x",) + tuple(range(PIECES))]:
        load(what, k).start()

    barrier = pltpu.get_barrier_semaphore()
    for device in [partner] + near + far:
        pl.semaphore_signal(barrier, inc=1, device_id=device, device_id_type=MESH)

    @pl.when(core == 1)
    def _():
        for device in near_0:
            pl.semaphore_signal(barrier, inc=1, device_id=device, device_id_type=MESH)

    def send(src, dst, k, device, recv=None):
        pltpu.make_async_remote_copy(
            src_ref=src, dst_ref=dst, send_sem=send_sem.at[k], recv_sem=recv_sem.at[k if recv is None else recv],
            device_id=device, device_id_type=MESH,
        ).start()

    def arrived(ref, k):
        pltpu.make_async_copy(ref, ref, recv_sem.at[k]).wait()

    def sent(ref, k):
        pltpu.make_async_copy(ref, ref, send_sem.at[k]).wait()

    xcol, xrow = place((RANK, PIX), 1)

    load("q", 0).wait()

    @pl.loop(0, 2)
    def _(k):
        layer = layer_of(k)
        q = halves(qv[layer])
        load("g", k).wait()
        u = dot_nt(q, gv[layer])
        u = u[:RANK] + u[RANK:]
        parts = []
        for a in range(3):
            for b in range(3):
                shift = SIDE * (a - 1) + (b - 1)
                part = pltpu.roll(u, shift % PIX, 1) if shift else u
                ok = None
                for tap, pos in ((a, xrow), (b, xcol)):
                    if tap != 1:
                        here = pos < SIDE - 1.5 if tap == 0 else pos > 0.5
                        ok = here if ok is None else jnp.logical_and(ok, here)
                parts.append(part if ok is None else jnp.where(ok, part, 0.0))
        ws[k] = halves(jnp.concatenate(parts, axis=0))

    @pl.loop(0, 2)
    def _(k):
        layer = layer_of(k)
        q = halves(qv[layer])
        load("x", k).wait()
        pg = dot(ws[k], xv[layer])
        pg = (pg[: 9 * RANK] + pg[9 * RANK :]) * grad_scale
        for n in range(PIECES):
            load(n, k).wait()
            pe = dot_nt(q, ev[layer, n * PROWS : (n + 1) * PROWS])
            pe = pe[:RANK] + pe[RANK:]
            for i in range(PROWS // 128):
                t = n * (PROWS // 128) + i
                tap, part = divmod(t, 4)
                tile = pe[:, 128 * i : 128 * i + 128] + pg[RANK * tap : RANK * tap + RANK, 128 * part : 128 * part + 128]
                for r in range(4):
                    pbuf[k, r * 4 + t // 9, t % 9] = tile[2 * r : 2 * r + 2]

        @pl.when(k == 0)
        def _():
            pl.semaphore_wait(barrier, 23 + 15 * core)
            send(pbuf.at[0], prx, 0, partner)

    arrived(prx, 0)
    psum[...] = pbuf[1] + prx[...]

    for t, device in zip(chips, near):
        send(psum.at[t], rs_rx.at[core, chip], 1, device, 10 + core)

    @pl.when(core == 0)
    def _():
        send(psum.at[chip], rs_rx.at[0, chip], 1, partner, 10)

    @pl.when(core == 1)
    def _():
        rs_rx[1, chip] = psum[chip]

    gpad[:, :, :SIDE] = jnp.zeros((3, 2, SIDE, COUT), f32)
    gpad[:, :, SIDE + IMG :] = jnp.zeros((3, 2, SIDE, COUT), f32)

    def prepare(layer):
        xt[...] = jnp.transpose(xv[layer])
        gcol, _ = place((PIX, COUT), 0)
        g = gv[layer].astype(f32)
        for b in range(3):
            if b == 1:
                part = g
            elif b == 0:
                part = jnp.where(gcol < SIDE - 1.5, pltpu.roll(g, PIX - 1, 0), 0.0)
            else:
                part = jnp.where(gcol > 0.5, pltpu.roll(g, 1, 0), 0.0)
            for i in range(2):
                gpad[b, i, SIDE : SIDE + IMG] = part[i * IMG : (i + 1) * IMG]

    def give(tap):
        rows = pl.ds(pl.multiple_of(tap * CIN, CIN), CIN)
        pltpu.make_async_remote_copy(
            src_ref=merged.at[other, rows], dst_ref=mrx.at[rows], send_sem=send_sem.at[9],
            recv_sem=piece_sem.at[tap], device_id=partner, device_id_type=MESH,
        ).start()

    @pl.loop(0, 6)
    def _(step):
        k = step // 3
        a = step - 3 * k
        layer = layer_of(k)

        @pl.when(a == 0)
        def _():
            prepare(layer)

        start = pl.multiple_of(2 * SIDE - SIDE * a, 8)
        for b in range(3):
            window = jnp.concatenate([gpad[b, i, pl.ds(start, IMG)] for i in range(2)], axis=0).astype(bf16)
            rows = pl.ds(pl.multiple_of((3 * a + b) * CIN, CIN), CIN)
            merged[layer, rows] = dot(xt[...], window) * grad_scale + ev[layer, rows].astype(f32)

        @pl.when(step == 0)
        def _():
            for n in range(3):
                give(n)

        @pl.when(step == 2)
        def _():
            for n in range(6, 8):
                give(n)

        @pl.when(k == 1)
        def _():
            for b in range(3):
                rows = pl.ds(pl.multiple_of((3 * a + b) * CIN, CIN), CIN)
                pltpu.make_async_copy(mrx.at[rows], mrx.at[rows], piece_sem.at[3 * a + b]).wait()
                both = merged[layer, rows] + mrx[rows]
                hi = both.astype(bf16)
                mhi[rows] = hi
                mlo[rows] = (both - hi.astype(f32)).astype(bf16)

        @pl.when(jnp.logical_and(step == AT_RS - 1, core == 1))
        def _():
            arrived(rs_rx.at[0], 10)
            arrived(rs_rx.at[1, pl.ds(0, 15)], 11)
            for i in range(LAYERS):
                part = rs_rx[i, 0]
                for n in range(1, NXY):
                    part = part + rs_rx[i, n]
                zbuf[z, i] = part

            for device in far:
                send(zbuf.at[z], zbuf.at[z], 2, device)

        @pl.when(step == AT_RS - 1)
        def _():
            for n in range(3, 6):
                give(n)

        @pl.when(jnp.logical_and(step == AT_Z - 1, core == 1))
        def _():
            arrived(zbuf.at[pl.ds(0, 7)], 2)
            for i in range(LAYERS):
                part = zbuf[0, i]
                for n in range(1, NZ):
                    part = part + zbuf[n, i]
                part = part * (1.0 / 256.0)
                if i == 0:
                    pown[...] = part
                else:
                    pfull[chip] = part

            def spread(src, k, device):
                pltpu.make_async_remote_copy(
                    src_ref=src, dst_ref=pfull.at[chip], send_sem=send_sem.at[k], recv_sem=line_sem.at[cy],
                    device_id=device, device_id_type=MESH,
                ).start()

            for device_0, device in zip(near_0, near):
                spread(pown, 10, device_0)
                spread(pfull.at[chip], 3, device)
            spread(pown, 10, partner)

        @pl.when(step == AT_Z - 1)
        def _():
            give(8)

    def line(n, total):
        y = lax.rem(cy + n + jnp.where(n == 2, 1, 0) - jnp.where(n == 3, 1, 0), 4)
        here = line_sem.at[y]

        mine = jnp.logical_and(n == 0, core == 1)

        @pl.when(mine)
        def _():
            pltpu.make_async_copy(pfull.at[pl.ds(0, 3)], pfull.at[pl.ds(0, 3)], here).wait()

        @pl.when(jnp.logical_not(mine))
        def _():
            pltpu.make_async_copy(pfull.at[pl.ds(0, 4)], pfull.at[pl.ds(0, 4)], here).wait()

        tiles = pl.ds(9 * y, 9)
        for r in range(4):
            pex[tiles, 2 * r : 2 * r + 2, :] = pfull[4 * r + y]
        left = halves(jnp.concatenate([pex[9 * y + i] for i in range(9)], axis=1))
        rows = pl.ds(pl.multiple_of(y * (KDIM // 4), KDIM // 4), KDIM // 4)
        return total + dot(left, mhi[rows]) + dot(left, mlo[rows])

    right = lax.fori_loop(0, 4, line, jnp.zeros((2 * RANK, COUT), f32))
    qx[core, chip] = right[:RANK] + right[RANK:]
    for device in near:
        send(qx.at[core, chip], qx.at[core, chip], 6, device, 12 + core)

    @pl.when(core == 0)
    def _():
        send(qx.at[0, chip], qx.at[0, chip], 6, partner, 12)

    unit = lax.broadcasted_iota(jnp.int32, (1, RANK, 128), 1) == lax.broadcasted_iota(jnp.int32, (1, RANK, 128), 2)
    unit = jnp.where(unit, 1.0, 0.0).astype(f32)
    (done,) = orthonormal([jnp.concatenate([pex[...], unit], axis=0)])
    ph[core] = done[:TILES]
    send(ph.at[core], ph.at[core], 4, partner)
    for s in range(RANK):
        rowop[core, s] = jnp.broadcast_to(done[TILES][:, s : s + 1], (RANK, COUT))
    send(rowop.at[core], rowop.at[core], 5, partner)

    def for_tail(layer):
        for t in range(0, TILES, 4):
            v = jnp.concatenate([ph[layer, t + k] for k in range(4)], axis=1)
            ph_out[layer, :, 128 * t : 128 * t + 512] = v
            hi = v.astype(bf16).astype(f32)
            both = jnp.concatenate([hi, v - hi, hi, jnp.zeros_like(hi)], axis=0)
            amat[layer, 128 * t : 128 * t + 512] = jnp.transpose(both).astype(bf16)

    for_tail(core)
    @pl.when(core == 1)
    def _():
        arrived(qx.at[0], 12)
        arrived(qx.at[1, pl.ds(0, 15)], 13)
        for i in range(LAYERS):
            part = qx[i, 0]
            for n in range(1, NXY):
                part = part + qx[i, n]
            qz[z, i] = part
        for device in far:
            send(qz.at[z], qz.at[z], 7, device)
        send(qz.at[z], qz.at[z], 8, partner)

    @pl.when(core == 0)
    def _():
        arrived(qz.at[0], 8)
        for device in far:
            send(qz.at[z], qz.at[z], 7, device)

    arrived(ph.at[0], 4)
    arrived(rowop.at[0], 5)
    for_tail(other)
    sent(pbuf.at[0], 0)
    sent(ph.at[0], 4)
    sent(rowop.at[0], 5)
    sent(merged.at[0], 9)

    @pl.when(core == 0)
    def _():
        sent(psum, 1)
        sent(qx.at[0], 6)

    @pl.when(core == 1)
    def _():
        sent(psum.at[pl.ds(0, 15)], 1)
        sent(zbuf.at[pl.ds(0, 7)], 2)
        sent(pfull.at[pl.ds(0, 15)], 3)
        sent(pfull, 10)
        sent(qx.at[0, pl.ds(0, 15)], 6)
        sent(qz.at[0], 8)

    sent(qz.at[pl.ds(0, 7)], 7)
    arrived(qz.at[pl.ds(0, 7)], 7)
    for i in range(LAYERS):
        part = qz[0, i]
        for n in range(1, NZ):
            part = part + qz[n, i]
        part = part * (1.0 / 256.0)
        right = rowop[i, 0] * part[0:1]
        for s in range(1, RANK):
            right = right + rowop[i, s] * part[s : s + 1]
        q_out[i] = right


CHUNK = 256


def tail_kernel(merged, amat, ph, q, p_hbm, q_hbm, e_hbm, stage, sem):
    outs = [pltpu.make_async_copy(ph, p_hbm, sem.at[0]), pltpu.make_async_copy(q, q_hbm, sem.at[1])]
    for copy in outs:
        copy.start()
    for layer in range(LAYERS):
        qh = q[layer]
        hi = qh.astype(bf16).astype(f32)
        right = jnp.concatenate([hi, hi, qh - hi, jnp.zeros_like(hi)], axis=0).astype(bf16)
        for c in range(KDIM // CHUNK):
            rows = slice(c * CHUNK, (c + 1) * CHUNK)
            low = dot(amat[layer, rows], right)
            stage[layer, rows] = (merged[layer, rows] - low).astype(bf16)
            copy = pltpu.make_async_copy(stage.at[layer, rows], e_hbm.at[layer, rows], sem.at[2 + layer * (KDIM // CHUNK) + c])
            copy.start()
            outs.append(copy)
    for copy in outs:
        copy.wait()


def body(activations, out_grads, errors, q_start):
    x = activations.reshape(LAYERS, PIX, CIN)
    g = out_grads.reshape(LAYERS, PIX, COUT)
    q0 = jnp.transpose(q_start, (0, 2, 1))
    x, g, errors, q0 = (pltpu.with_memory_space_constraint(a, pltpu.HBM) for a in (x, g, errors, q0))
    hbm = pl.BlockSpec(memory_space=pltpu.HBM)
    vmem = pl.BlockSpec(memory_space=pltpu.VMEM)
    V = pltpu.VMEM
    chunks = (9, 2, 128)
    merged, amat, ph, q = pl.pallas_call(
        main_kernel,
        out_shape=[
            V((LAYERS, KDIM, COUT), f32),
            V((LAYERS, KDIM, 4 * RANK), bf16),
            V((LAYERS, RANK, KDIM), f32),
            V((LAYERS, RANK, COUT), f32),
        ],
        in_specs=[hbm] * 4,
        out_specs=[vmem] * 4,
        scratch_shapes=[
            V((LAYERS, PIX, CIN), bf16),
            V((LAYERS, PIX, COUT), bf16),
            V((LAYERS, KDIM, COUT), bf16),
            V((LAYERS, RANK, COUT), f32),
            V((CIN, PIX), bf16),
            V((3, 2, IMG + 2 * SIDE, COUT), f32),
            V((KDIM, COUT), bf16),
            V((KDIM, COUT), bf16),
            V((2, 2 * 9 * RANK, PIX), bf16),
            V((2, NXY) + chunks, f32),
            V((NXY,) + chunks, f32),
            V((NXY,) + chunks, f32),
            V((LAYERS, NXY) + chunks, f32),
            V((NZ, LAYERS) + chunks, f32),
            V(chunks, f32),
            V((NXY,) + chunks, f32),
            V((TILES, RANK, 128), f32),
            V((LAYERS, TILES, RANK, 128), f32),
            V((LAYERS, RANK, RANK, COUT), f32),
            V((KDIM, COUT), f32),
            V((LAYERS, NXY, RANK, COUT), f32),
            V((NZ, LAYERS, RANK, COUT), f32),
            pltpu.SemaphoreType.DMA((11,)),
            pltpu.SemaphoreType.DMA((11,)),
            pltpu.SemaphoreType.DMA((14,)),
            pltpu.SemaphoreType.DMA((9,)),
            pltpu.SemaphoreType.DMA((4,)),
        ],
        compiler_params=pltpu.CompilerParams(
            collective_id=0, has_side_effects=True, vmem_limit_bytes=32 << 20
        ),
        cost_estimate=pl.CostEstimate(flops=2 * 2 * KDIM * PIX * COUT, bytes_accessed=9 << 20, transcendentals=0),
        name="factors",
    )(x, g, errors, q0)
    p_t, q_t, new_errors = pl.pallas_call(
        tail_kernel,
        out_shape=[
            jax.ShapeDtypeStruct((LAYERS, RANK, KDIM), f32),
            jax.ShapeDtypeStruct((LAYERS, RANK, COUT), f32),
            jax.ShapeDtypeStruct((LAYERS, KDIM, COUT), bf16),
        ],
        in_specs=[vmem] * 4,
        out_specs=[hbm] * 3,
        scratch_shapes=[V((LAYERS, KDIM, COUT), bf16), pltpu.SemaphoreType.DMA((2 + 2 * (KDIM // CHUNK),))],
        compiler_params=pltpu.CompilerParams(vmem_limit_bytes=32 << 20),
        cost_estimate=pl.CostEstimate(flops=2 * 2 * KDIM * 32 * COUT, bytes_accessed=5 << 20, transcendentals=0),
        name="memory_update",
    )(merged, amat, ph, q)
    return jnp.transpose(p_t, (0, 2, 1)), jnp.transpose(q_t, (0, 2, 1)), new_errors


def solution(mesh):
    placed = (
        P(None, ("row", "col"), None, None, None),
        P(None, ("row", "col"), None, None, None),
        P(None, ("row", "col"), None),
        P(),
    )
    return jax.shard_map(
        body,
        mesh=mesh,
        in_specs=placed,
        out_specs=(P(), P(), P(None, ("row", "col"), None)),
        check_vma=False,
    )
```

```python
import functools
import jax
import jax.numpy as jnp
from jax import lax
from jax.experimental import pallas as pl
from jax.experimental.pallas import tpu as pltpu
from jax.sharding import PartitionSpec as P

grad_scale = 0.03125
epsilon = 1e-06
f32 = jnp.float32
bf16 = jnp.bfloat16
MESH = pl.DeviceIdType.MESH

LAYERS, SIDE, PIX, CIN, COUT, RANK, KDIM = 2, 24, 1152, 512, 256, 8, 4608
IMG = SIDE * SIDE
TILES = KDIM // 128
NXY, NZ = 16, 8


def halves(v):
    hi = v.astype(bf16).astype(f32)
    return jnp.concatenate([hi, v - hi], axis=0).astype(bf16)


def dot_nt(a, b):
    return lax.dot_general(a, b, (((1,), (1,)), ((), ())), preferred_element_type=f32)


def dot(a, b):
    return jnp.dot(a, b, preferred_element_type=f32)


def place(shape, axis):
    pix = lax.broadcasted_iota(jnp.int32, shape, axis).astype(f32)
    line = jnp.floor((pix + 0.5) * (1.0 / SIDE))
    col = pix - line * SIDE
    row = line - jnp.floor((line + 0.5) * (1.0 / SIDE)) * SIDE
    return col, row


def orthonormal(layers):
    rank = lax.broadcasted_iota(jnp.int32, (1, RANK, 1), 1)
    layers = list(layers)
    scales = [jnp.zeros((1, RANK, 1), f32) for _ in layers]
    for j in range(RANK):
        for k, c in enumerate(layers):
            cj = c[:, j : j + 1, :]
            prod = c[:TILES] * cj[:TILES]
            dots = jnp.sum(jnp.sum(prod, axis=0, keepdims=True), axis=2, keepdims=True)
            square = dots[:, j : j + 1, :] + epsilon
            scales[k] = jnp.where(rank == j, 1.0 / jnp.sqrt(square), scales[k])
            if j < RANK - 1:
                layers[k] = c - jnp.where(rank > j, dots / square, 0.0) * cj
    return [c * scale for c, scale in zip(layers, scales)]


def far_first(offsets, sizes):
    return sorted(offsets, key=lambda d: -sum(min(i, n - i) for i, n in zip(d, sizes)))


NEAR = far_first([(i, j) for i in range(4) for j in range(4) if i or j], (4, 4))
FAR = far_first([(k,) for k in range(1, NZ)], (NZ,))
PIECES = 1
PROWS = KDIM // PIECES
AT_RS, AT_Z = 2, 4


def main_kernel(
    x_hbm, g_hbm, e_hbm, q0_hbm,
    merged, amat, ph_out, q_out,
    xv, gv, ev, qv, xt, gpad, mhi, mlo,
    ws, pbuf, prx, psum, rs_rx, zbuf, pown, pfull, pex, ph, rowop,
    mrx, qx, qz,
    load_sem, send_sem, recv_sem, piece_sem, line_sem,
):
    z = lax.axis_index("row")
    col = lax.axis_index("col")
    core = lax.rem(col, 2)
    chip = col // 2
    other = 1 - core
    partner = (z, chip * 2 + other)
    cx, cy = chip // 4, lax.rem(chip, 4)
    chips = [lax.rem(cx + i, 4) * 4 + lax.rem(cy + j, 4) for i, j in NEAR]
    near = [(z, t * 2 + 1) for t in chips]
    near_0 = [(z, t * 2) for t in chips]
    far = [(lax.rem(z + k, NZ), col) for (k,) in FAR]

    def layer_of(k):
        return other + k * (core - other)

    def load(what, k):
        layer = layer_of(k)
        if what == "q":
            return pltpu.make_async_copy(q0_hbm, qv, load_sem.at[0])
        if what == "g":
            return pltpu.make_async_copy(g_hbm.at[layer], gv.at[layer], load_sem.at[1 + k])
        if what == "x":
            return pltpu.make_async_copy(x_hbm.at[layer], xv.at[layer], load_sem.at[3 + k])
        rows = pl.ds(what * PROWS, PROWS)
        return pltpu.make_async_copy(e_hbm.at[layer, rows], ev.at[layer, rows], load_sem.at[5 + 2 * what + k])

    load("q", 0).start()
    for what, k in [("g", 0), ("g", 1)] + [(what, k) for k in range(2) for what in ("x",) + tuple(range(PIECES))]:
        load(what, k).start()

    barrier = pltpu.get_barrier_semaphore()
    for device in [partner] + near + far:
        pl.semaphore_signal(barrier, inc=1, device_id=device, device_id_type=MESH)

    @pl.when(core == 1)
    def _():
        for device in near_0:
            pl.semaphore_signal(barrier, inc=1, device_id=device, device_id_type=MESH)

    def send(src, dst, k, device, recv=None):
        pltpu.make_async_remote_copy(
            src_ref=src, dst_ref=dst, send_sem=send_sem.at[k], recv_sem=recv_sem.at[k if recv is None else recv],
            device_id=device, device_id_type=MESH,
        ).start()

    def arrived(ref, k):
        pltpu.make_async_copy(ref, ref, recv_sem.at[k]).wait()

    def sent(ref, k):
        pltpu.make_async_copy(ref, ref, send_sem.at[k]).wait()

    xcol, xrow = place((RANK, PIX), 1)

    load("q", 0).wait()

    @pl.loop(0, 2)
    def _(k):
        layer = layer_of(k)
        q = halves(qv[layer])
        load("g", k).wait()
        u = dot_nt(q, gv[layer])
        u = u[:RANK] + u[RANK:]
        parts = []
        for a in range(3):
            for b in range(3):
                shift = SIDE * (a - 1) + (b - 1)
                part = pltpu.roll(u, shift % PIX, 1) if shift else u
                ok = None
                for tap, pos in ((a, xrow), (b, xcol)):
                    if tap != 1:
                        here = pos < SIDE - 1.5 if tap == 0 else pos > 0.5
                        ok = here if ok is None else jnp.logical_and(ok, here)
                parts.append(part if ok is None else jnp.where(ok, part, 0.0))
        ws[k] = halves(jnp.concatenate(parts, axis=0))

    @pl.loop(0, 2)
    def _(k):
        layer = layer_of(k)
        q = halves(qv[layer])
        load("x", k).wait()
        pg = dot(ws[k], xv[layer])
        pg = (pg[: 9 * RANK] + pg[9 * RANK :]) * grad_scale
        for n in range(PIECES):
            load(n, k).wait()
            pe = dot_nt(q, ev[layer, n * PROWS : (n + 1) * PROWS])
            pe = pe[:RANK] + pe[RANK:]
            for i in range(PROWS // 128):
                t = n * (PROWS // 128) + i
                tap, part = divmod(t, 4)
                tile = pe[:, 128 * i : 128 * i + 128] + pg[RANK * tap : RANK * tap + RANK, 128 * part : 128 * part + 128]
                for r in range(4):
                    pbuf[k, r * 4 + t // 9, t % 9] = tile[2 * r : 2 * r + 2]

        @pl.when(k == 0)
        def _():
            pl.semaphore_wait(barrier, 23 + 15 * core)
            send(pbuf.at[0], prx, 0, partner)

    arrived(prx, 0)
    psum[...] = pbuf[1] + prx[...]

    for t, device in zip(chips, near):
        send(psum.at[t], rs_rx.at[core, chip], 1, device, 10 + core)

    @pl.when(core == 0)
    def _():
        send(psum.at[chip], rs_rx.at[0, chip], 1, partner, 10)

    @pl.when(core == 1)
    def _():
        rs_rx[1, chip] = psum[chip]

    gpad[:, :, :SIDE] = jnp.zeros((3, 2, SIDE, COUT), f32)
    gpad[:, :, SIDE + IMG :] = jnp.zeros((3, 2, SIDE, COUT), f32)

    def prepare(layer):
        gcol, _ = place((PIX, COUT), 0)
        g = gv[layer].astype(f32)
        for b in range(3):
            if b == 1:
                part = g
            elif b == 0:
                part = jnp.where(gcol < SIDE - 1.5, pltpu.roll(g, PIX - 1, 0), 0.0)
            else:
                part = jnp.where(gcol > 0.5, pltpu.roll(g, 1, 0), 0.0)
            for i in range(2):
                gpad[b, i, SIDE : SIDE + IMG] = part[i * IMG : (i + 1) * IMG]

    def give(tap):
        rows = pl.ds(pl.multiple_of(tap * CIN, CIN), CIN)
        pltpu.make_async_remote_copy(
            src_ref=merged.at[other, rows], dst_ref=mrx.at[rows], send_sem=send_sem.at[9],
            recv_sem=piece_sem.at[tap], device_id=partner, device_id_type=MESH,
        ).start()

    @pl.loop(0, 6)
    def _(step):
        k = step // 3
        a = step - 3 * k
        layer = layer_of(k)

        @pl.when(step == 0)
        def _():
            for i in range(LAYERS):
                xt[i] = jnp.transpose(xv[i])

        @pl.when(a == 0)
        def _():
            prepare(layer)

        start = pl.multiple_of(2 * SIDE - SIDE * a, 8)
        for b in range(3):
            window = jnp.concatenate([gpad[b, i, pl.ds(start, IMG)] for i in range(2)], axis=0).astype(bf16)
            rows = pl.ds(pl.multiple_of((3 * a + b) * CIN, CIN), CIN)
            merged[layer, rows] = dot(xt[layer], window) * grad_scale + ev[layer, rows].astype(f32)

        @pl.when(step == 0)
        def _():
            for n in range(3):
                give(n)

        @pl.when(step == 2)
        def _():
            for n in range(6, 8):
                give(n)

        @pl.when(k == 1)
        def _():
            for b in range(3):
                rows = pl.ds(pl.multiple_of((3 * a + b) * CIN, CIN), CIN)
                pltpu.make_async_copy(mrx.at[rows], mrx.at[rows], piece_sem.at[3 * a + b]).wait()
                both = merged[layer, rows] + mrx[rows]
                hi = both.astype(bf16)
                mhi[rows] = hi
                mlo[rows] = (both - hi.astype(f32)).astype(bf16)

        @pl.when(jnp.logical_and(step == AT_RS - 1, core == 1))
        def _():
            arrived(rs_rx.at[0], 10)
            arrived(rs_rx.at[1, pl.ds(0, 15)], 11)
            for i in range(LAYERS):
                part = rs_rx[i, 0]
                for n in range(1, NXY):
                    part = part + rs_rx[i, n]
                zbuf[z, i] = part

            for device in far:
                send(zbuf.at[z], zbuf.at[z], 2, device)

        @pl.when(step == AT_RS - 1)
        def _():
            for n in range(3, 6):
                give(n)

        @pl.when(jnp.logical_and(step == AT_Z - 1, core == 1))
        def _():
            arrived(zbuf.at[pl.ds(0, 7)], 2)
            for i in range(LAYERS):
                part = zbuf[0, i]
                for n in range(1, NZ):
                    part = part + zbuf[n, i]
                part = part * (1.0 / 256.0)
                if i == 0:
                    pown[...] = part
                else:
                    pfull[chip] = part

            def spread(src, k, device):
                pltpu.make_async_remote_copy(
                    src_ref=src, dst_ref=pfull.at[chip], send_sem=send_sem.at[k], recv_sem=line_sem.at[cy],
                    device_id=device, device_id_type=MESH,
                ).start()

            for device_0, device in zip(near_0, near):
                spread(pown, 10, device_0)
                spread(pfull.at[chip], 3, device)
            spread(pown, 10, partner)

        @pl.when(step == AT_Z - 1)
        def _():
            give(8)

    def line(n, total):
        y = lax.rem(cy + n + jnp.where(n == 2, 1, 0) - jnp.where(n == 3, 1, 0), 4)
        here = line_sem.at[y]

        mine = jnp.logical_and(n == 0, core == 1)

        @pl.when(mine)
        def _():
            pltpu.make_async_copy(pfull.at[pl.ds(0, 3)], pfull.at[pl.ds(0, 3)], here).wait()

        @pl.when(jnp.logical_not(mine))
        def _():
            pltpu.make_async_copy(pfull.at[pl.ds(0, 4)], pfull.at[pl.ds(0, 4)], here).wait()

        tiles = pl.ds(9 * y, 9)
        for r in range(4):
            pex[tiles, 2 * r : 2 * r + 2, :] = pfull[4 * r + y]
        left = halves(jnp.concatenate([pex[9 * y + i] for i in range(9)], axis=1))
        rows = pl.ds(pl.multiple_of(y * (KDIM // 4), KDIM // 4), KDIM // 4)
        return total + dot(left, mhi[rows]) + dot(left, mlo[rows])

    right = lax.fori_loop(0, 4, line, jnp.zeros((2 * RANK, COUT), f32))
    qx[core, chip] = right[:RANK] + right[RANK:]
    for device in near:
        send(qx.at[core, chip], qx.at[core, chip], 6, device, 12 + core)

    @pl.when(core == 0)
    def _():
        send(qx.at[0, chip], qx.at[0, chip], 6, partner, 12)

    unit = lax.broadcasted_iota(jnp.int32, (1, RANK, 128), 1) == lax.broadcasted_iota(jnp.int32, (1, RANK, 128), 2)
    unit = jnp.where(unit, 1.0, 0.0).astype(f32)
    (done,) = orthonormal([jnp.concatenate([pex[...], unit], axis=0)])
    ph[core] = done[:TILES]
    send(ph.at[core], ph.at[core], 4, partner)
    for s in range(RANK):
        rowop[core, s] = jnp.broadcast_to(done[TILES][:, s : s + 1], (RANK, COUT))
    send(rowop.at[core], rowop.at[core], 5, partner)

    def for_tail(layer):
        for t in range(0, TILES, 4):
            v = jnp.concatenate([ph[layer, t + k] for k in range(4)], axis=1)
            ph_out[layer, :, 128 * t : 128 * t + 512] = v
            hi = v.astype(bf16).astype(f32)
            both = jnp.concatenate([hi, v - hi, hi, jnp.zeros_like(hi)], axis=0)
            amat[layer, 128 * t : 128 * t + 512] = jnp.transpose(both).astype(bf16)

    for_tail(core)
    @pl.when(core == 1)
    def _():
        arrived(qx.at[0], 12)
        arrived(qx.at[1, pl.ds(0, 15)], 13)
        for i in range(LAYERS):
            part = qx[i, 0]
            for n in range(1, NXY):
                part = part + qx[i, n]
            qz[z, i] = part
        for device in far:
            send(qz.at[z], qz.at[z], 7, device)
        send(qz.at[z], qz.at[z], 8, partner)

    @pl.when(core == 0)
    def _():
        arrived(qz.at[0], 8)
        for device in far:
            send(qz.at[z], qz.at[z], 7, device)

    arrived(ph.at[0], 4)
    arrived(rowop.at[0], 5)
    for_tail(other)
    sent(pbuf.at[0], 0)
    sent(ph.at[0], 4)
    sent(rowop.at[0], 5)
    sent(merged.at[0], 9)

    @pl.when(core == 0)
    def _():
        sent(psum, 1)
        sent(qx.at[0], 6)

    @pl.when(core == 1)
    def _():
        sent(psum.at[pl.ds(0, 15)], 1)
        sent(zbuf.at[pl.ds(0, 7)], 2)
        sent(pfull.at[pl.ds(0, 15)], 3)
        sent(pfull, 10)
        sent(qx.at[0, pl.ds(0, 15)], 6)
        sent(qz.at[0], 8)

    sent(qz.at[pl.ds(0, 7)], 7)
    arrived(qz.at[pl.ds(0, 7)], 7)
    for i in range(LAYERS):
        part = qz[0, i]
        for n in range(1, NZ):
            part = part + qz[n, i]
        part = part * (1.0 / 256.0)
        right = rowop[i, 0] * part[0:1]
        for s in range(1, RANK):
            right = right + rowop[i, s] * part[s : s + 1]
        q_out[i] = right


CHUNK = 256


def tail_kernel(merged, amat, ph, q, p_hbm, q_hbm, e_hbm, stage, sem):
    outs = [pltpu.make_async_copy(ph, p_hbm, sem.at[0]), pltpu.make_async_copy(q, q_hbm, sem.at[1])]
    for copy in outs:
        copy.start()
    for layer in range(LAYERS):
        qh = q[layer]
        hi = qh.astype(bf16).astype(f32)
        right = jnp.concatenate([hi, hi, qh - hi, jnp.zeros_like(hi)], axis=0).astype(bf16)
        for c in range(KDIM // CHUNK):
            rows = slice(c * CHUNK, (c + 1) * CHUNK)
            low = dot(amat[layer, rows], right)
            stage[layer, rows] = (merged[layer, rows] - low).astype(bf16)
            copy = pltpu.make_async_copy(stage.at[layer, rows], e_hbm.at[layer, rows], sem.at[2 + layer * (KDIM // CHUNK) + c])
            copy.start()
            outs.append(copy)
    for copy in outs:
        copy.wait()


def body(activations, out_grads, errors, q_start):
    x = activations.reshape(LAYERS, PIX, CIN)
    g = out_grads.reshape(LAYERS, PIX, COUT)
    q0 = jnp.transpose(q_start, (0, 2, 1))
    x, g, errors, q0 = (pltpu.with_memory_space_constraint(a, pltpu.HBM) for a in (x, g, errors, q0))
    hbm = pl.BlockSpec(memory_space=pltpu.HBM)
    vmem = pl.BlockSpec(memory_space=pltpu.VMEM)
    V = pltpu.VMEM
    chunks = (9, 2, 128)
    merged, amat, ph, q = pl.pallas_call(
        main_kernel,
        out_shape=[
            V((LAYERS, KDIM, COUT), f32),
            V((LAYERS, KDIM, 4 * RANK), bf16),
            V((LAYERS, RANK, KDIM), f32),
            V((LAYERS, RANK, COUT), f32),
        ],
        in_specs=[hbm] * 4,
        out_specs=[vmem] * 4,
        scratch_shapes=[
            V((LAYERS, PIX, CIN), bf16),
            V((LAYERS, PIX, COUT), bf16),
            V((LAYERS, KDIM, COUT), bf16),
            V((LAYERS, RANK, COUT), f32),
            V((LAYERS, CIN, PIX), bf16),
            V((3, 2, IMG + 2 * SIDE, COUT), f32),
            V((KDIM, COUT), bf16),
            V((KDIM, COUT), bf16),
            V((2, 2 * 9 * RANK, PIX), bf16),
            V((2, NXY) + chunks, f32),
            V((NXY,) + chunks, f32),
            V((NXY,) + chunks, f32),
            V((LAYERS, NXY) + chunks, f32),
            V((NZ, LAYERS) + chunks, f32),
            V(chunks, f32),
            V((NXY,) + chunks, f32),
            V((TILES, RANK, 128), f32),
            V((LAYERS, TILES, RANK, 128), f32),
            V((LAYERS, RANK, RANK, COUT), f32),
            V((KDIM, COUT), f32),
            V((LAYERS, NXY, RANK, COUT), f32),
            V((NZ, LAYERS, RANK, COUT), f32),
            pltpu.SemaphoreType.DMA((11,)),
            pltpu.SemaphoreType.DMA((11,)),
            pltpu.SemaphoreType.DMA((14,)),
            pltpu.SemaphoreType.DMA((9,)),
            pltpu.SemaphoreType.DMA((4,)),
        ],
        compiler_params=pltpu.CompilerParams(
            collective_id=0, has_side_effects=True, vmem_limit_bytes=32 << 20
        ),
        cost_estimate=pl.CostEstimate(flops=2 * 2 * KDIM * PIX * COUT, bytes_accessed=9 << 20, transcendentals=0),
        name="factors",
    )(x, g, errors, q0)
    p_t, q_t, new_errors = pl.pallas_call(
        tail_kernel,
        out_shape=[
            jax.ShapeDtypeStruct((LAYERS, RANK, KDIM), f32),
            jax.ShapeDtypeStruct((LAYERS, RANK, COUT), f32),
            jax.ShapeDtypeStruct((LAYERS, KDIM, COUT), bf16),
        ],
        in_specs=[vmem] * 4,
        out_specs=[hbm] * 3,
        scratch_shapes=[V((LAYERS, KDIM, COUT), bf16), pltpu.SemaphoreType.DMA((2 + 2 * (KDIM // CHUNK),))],
        compiler_params=pltpu.CompilerParams(vmem_limit_bytes=32 << 20),
        cost_estimate=pl.CostEstimate(flops=2 * 2 * KDIM * 32 * COUT, bytes_accessed=5 << 20, transcendentals=0),
        name="memory_update",
    )(merged, amat, ph, q)
    return jnp.transpose(p_t, (0, 2, 1)), jnp.transpose(q_t, (0, 2, 1)), new_errors


def solution(mesh):
    placed = (
        P(None, ("row", "col"), None, None, None),
        P(None, ("row", "col"), None, None, None),
        P(None, ("row", "col"), None),
        P(),
    )
    return jax.shard_map(
        body,
        mesh=mesh,
        in_specs=placed,
        out_specs=(P(), P(), P(None, ("row", "col"), None)),
        check_vma=False,
    )
```
